32 devices in a mesh: row: 4 (over z), col: 2 (over y), win: 4 (over x, core).
Axes of the slice: x: 2, y: 2, z: 4, core: 2. Of those that a mesh axis runs over, the one named last changes fastest.
Arguments:
- counts: int32 [8, 512, 2048], P('win', 'row', 'col'), may hold values from 0 to 31, as said below
- row_factors: float32 [32, 512], P(None, ('row', 'col', 'win')), may hold values from 0.15 to 1.5
- col_factors: float32 [32, 2048], P(None, ('col', 'row', 'win')), may hold values from 0.15 to 1.5
- win_factors: float32 [32, 8], P(None, 'win'), may hold values from 0.15 to 1.5
Outputs:
- new_rows: float32 [32, 512], P(None, ('row', 'col', 'win'))
- new_cols: float32 [32, 2048], P(None, ('col', 'row', 'win'))
- new_wins: float32 [32, 8], P(None, 'win')
The draws below stay inside these ranges and needn't reach their ends.
Inputs may be any that keep to these rules, and one draw needn't show every extreme that they name: counts are whole numbers.
All inputs are finite; a program needn't handle non-finite values.
Results may differ from the reference program's by a relative error of at most 0.0001.
Values sent between devices are 32-bit elements; how exact they have to be, the bound alone decides.
A program may use at most 64 MiB of HBM per device.

```python
import math
import jax
import jax.numpy as jnp
from jax import lax

RANK = 32
STEPS = 4
NI = 512
NJ = 2048
NW = 8


def draw_counts(key, part):
    key_rows = jax.random.fold_in(key, 11)
    key_cols = jax.random.fold_in(key, 12)
    key_wins = jax.random.fold_in(key, 13)
    key_vals = jax.random.fold_in(key, 14)
    row_level = jax.random.randint(key_rows, (NI,), 0, 4)
    col_level = jax.random.randint(key_cols, (NJ,), 0, 4)
    win_level = jax.random.randint(key_wins, (NW,), 1, 4)
    top_value = 5 + win_level[:, None, None] * row_level[None, :, None] * col_level[None, None, :]
    values = jax.random.randint(key_vals, (NW, NI, NJ), 0, top_value)
    values = values.at[0, 0, 0].set(31)
    values = values.at[0, 0, 1].set(0)
    return values.astype(jnp.int32)


def levels(rng, extent, shards, least, high):
    level, own = 1.0, jax.random.fold_in(rng, 6)
    for axis_at, blocks in shards:
        heights = jnp.exp(jax.random.uniform(jax.random.fold_in(own, axis_at), (blocks,), jnp.float32, least / len(shards), high / len(shards)))
        level = level * jnp.repeat(heights, extent[axis_at] // blocks).reshape([-1 if axis == axis_at else 1 for axis in range(len(extent))])
    return level


def setup_inputs(seed: int = 0) -> dict:
    splits = jax.random.split(jax.random.key(seed), 5)
    counts = draw_counts(jax.random.fold_in(splits[4], 71), 0)
    row_factors = jnp.clip(jnp.exp(math.log(1.5) - 2.3025851 * jax.random.uniform(splits[1], (RANK, NI), jnp.float32) ** levels(splits[1], (RANK, NI), ((1, 32),), -0.2, 0.2)), 0.15, 1.5)
    col_factors = jnp.clip(jnp.exp(math.log(1.5) - 2.3025851 * jax.random.uniform(splits[2], (RANK, NJ), jnp.float32) ** levels(splits[2], (RANK, NJ), ((1, 32),), -0.2, 0.2)), 0.15, 1.5)
    win_factors = jnp.clip(jnp.exp(math.log(1.5) - 2.3025851 * jax.random.uniform(splits[3], (RANK, NW), jnp.float32) ** levels(splits[3], (RANK, NW), ((1, 4),), -0.2, 0.2)), 0.15, 1.5)
    return dict(counts=counts, row_factors=row_factors, col_factors=col_factors, win_factors=win_factors)


HIGH = lax.Precision.HIGHEST


def reference(counts, row_factors, col_factors, win_factors):
    rows_now = row_factors
    cols_now = col_factors
    wins_now = win_factors
    for step_index in range(STEPS):
        row_terms = jnp.zeros(rows_now.shape, jnp.float32)
        col_terms = jnp.zeros(cols_now.shape, jnp.float32)
        win_list = []
        for window in range(NW):
            weight = wins_now[:, window:window + 1]
            scaled = rows_now * weight
            model_block = lax.dot_general(scaled, cols_now, (((0,), (0,)), ((), ())), precision=HIGH, preferred_element_type=jnp.float32)
            count_ratio = counts[window].astype(jnp.float32) / model_block
            back_terms = lax.dot_general(cols_now, count_ratio, (((1,), (1,)), ((), ())), precision=HIGH, preferred_element_type=jnp.float32)
            row_terms = row_terms + back_terms * weight
            col_terms = col_terms + jnp.dot(scaled, count_ratio, precision=HIGH, preferred_element_type=jnp.float32)
            win_list.append(wins_now[:, window] * jnp.sum(rows_now * back_terms, axis=1))
        win_terms = jnp.stack(win_list, axis=1)
        sum_rows = jnp.sum(rows_now, axis=1)
        sum_cols = jnp.sum(cols_now, axis=1)
        sum_wins = jnp.sum(wins_now, axis=1)
        rows_next = rows_now * (0.5 + 0.5 * row_terms / (sum_cols * sum_wins)[:, None])
        cols_next = cols_now * (0.5 + 0.5 * col_terms / (sum_rows * sum_wins)[:, None])
        wins_next = wins_now * (0.5 + 0.5 * win_terms / (sum_rows * sum_cols)[:, None])
        rows_now, cols_now, wins_now = rows_next, cols_next, wins_next
    return rows_now, cols_now, wins_now
```

```python
import functools

import jax
import jax.numpy as jnp
from jax import lax
from jax.experimental import pallas as pl
from jax.experimental.pallas import tpu as pltpu
from jax.sharding import PartitionSpec as P

STEPS = 4
LANES = 128
MESH = pl.DeviceIdType.MESH
F32 = jnp.float32
BF16 = jnp.bfloat16


def dot(a, b):
    return lax.dot_general(a, b, (((1,), (0,)), ((), ())), preferred_element_type=F32)


def split(value):
    high = value.astype(BF16)
    low = (value - high.astype(F32)).astype(BF16)
    return high, low


def kernel(
    sizes,
    counts_ref, row_ref, col_ref, win_ref,
    row_out, col_out, win_out,
    cnt, cnt_send, a_now, b_now, c_now, scale_a, pa_now,
    ia, ib, pa_send, rr, pb_send, rc, ga, gb, zs,
    sems,
):
    nrow, ncol, nwin = sizes
    rank, row_width = row_ref.shape
    col_width = col_ref.shape[1]
    own_wins, items, columns = counts_ref.shape
    half = columns // 2
    nx = nwin // 2
    npr, npc = ncol * nwin, nrow * nx
    groups = half // LANES
    rk_r, rk_c = rank // npr, rank * groups // npc
    local_wins = 2 * own_wins

    row, col, win = lax.axis_index("row"), lax.axis_index("col"), lax.axis_index("win")
    xpos, core = win // 2, win % 2
    me_r = col * nwin + win
    me_c = row * nx + xpos

    def row_peer(d):
        q = (me_r + d) % npr
        return q, (row, q // nwin, q % nwin)

    def col_peer(d):
        q = (me_c + d) % npc
        return q, (q // nx, col, (q % nx) * 2 + core)

    def z_peer(d):
        q = (row + d) % nrow
        return q, (q, col, win)

    def remote(src, dst, kind, device):
        return pltpu.make_async_remote_copy(
            src_ref=src, dst_ref=dst, send_sem=sems.at[0, kind], recv_sem=sems.at[1, kind],
            device_id=device, device_id_type=MESH,
        )

    def wait_all(slots, kind, device):
        n = slots.shape[0] - 1
        part = slots.at[pl.ds(0, n)]
        both = remote(part, part, kind, device)
        both.wait_recv()

    def wait_sent(slots, kind, device):
        n = slots.shape[0] - 1
        part = slots.at[pl.ds(0, n)]
        remote(part, part, kind, device).wait_send()

    some_row, some_col, some_z = row_peer(1)[1], col_peer(1)[1], z_peer(1)[1]
    partner = (row, col, 2 * xpos + (1 - core))

    barrier = pltpu.get_barrier_semaphore()
    for d in range(1, npr):
        pl.semaphore_signal(barrier, inc=1, device_id=row_peer(d)[1], device_id_type=MESH)
    for d in range(1, npc):
        pl.semaphore_signal(barrier, inc=1, device_id=col_peer(d)[1], device_id_type=MESH)

    ia[me_r] = jnp.zeros((rank, LANES), F32)
    ia[me_r, :, 0:row_width] = row_ref[...]
    ia[me_r, :, row_width : row_width + own_wins] = win_ref[...]
    ib[me_c] = jnp.zeros((rank, LANES), F32)
    ib[me_c, :, 0:col_width] = col_ref[...]

    pl.semaphore_wait(barrier, npr - 1 + npc - 1)

    for d in range(1, npc):
        remote(ib.at[me_c], ib.at[me_c], 0, col_peer(d)[1]).start()
    for d in range(1, npr):
        remote(ia.at[me_r], ia.at[me_r], 1, row_peer(d)[1]).start()

    span = 2 * LANES
    src_at = lax.broadcasted_iota(jnp.int32, (span, span), 0)
    dst_at = lax.broadcasted_iota(jnp.int32, (span, span), 1)
    side = dst_at // LANES
    lane = dst_at % LANES
    take = jnp.where(side == 0, core, 1 - core)
    origin = (lane // col_width) * (2 * col_width) + take * col_width + lane % col_width
    order = jnp.where(src_at == origin, 1.0, 0.0).astype(BF16)
    base = core * (own_wins * items)
    for w in range(own_wins):
        for g in range(groups):
            block = counts_ref[w, :, g * span : (g + 1) * span].astype(F32).astype(BF16)
            moved = dot(block, order)
            at = pl.ds(pl.multiple_of(base + w * items, items), items)
            cnt[at, g * LANES : (g + 1) * LANES] = moved[:, :LANES]
            cnt_send[w * items : (w + 1) * items, g * LANES : (g + 1) * LANES] = moved[:, LANES:]
    mine = cnt.at[pl.ds(pl.multiple_of(base, items), own_wins * items)]
    swap = remote(cnt_send, mine, 2, partner)
    swap.start()

    lane_at = lax.broadcasted_iota(jnp.int32, (rank, LANES), 1)
    row_at = lax.broadcasted_iota(jnp.int32, (LANES, LANES), 0)

    wait_all(ib, 0, some_col)
    per = LANES // col_width
    for g in range(groups):
        block = ib[g * per]
        for m in range(1, per):
            moved = pltpu.roll(ib[g * per + m], m * col_width, 1)
            block = jnp.where(lane_at // col_width == m, moved, block)
        b_now[:, g * LANES : (g + 1) * LANES] = block
    wait_all(ia, 1, some_row)
    block = ia[0]
    for m in range(1, npr):
        moved = pltpu.roll(ia[m], m * row_width, 1)
        block = jnp.where(lane_at // row_width == m, moved, block)
    a_now[...] = block
    wins = jnp.zeros((rank, LANES), F32)
    for w in range(nwin):
        moved = pltpu.roll(ia[w], (LANES - row_width + w * own_wins) % LANES, 1)
        wins = jnp.where(lane_at // own_wins == w, moved, wins)
    pad = jnp.zeros((LANES - rank, LANES), F32)
    c_now[...] = jnp.transpose(jnp.concatenate([wins, pad], axis=0))[: nwin * own_wins]
    wait_sent(ib, 0, some_col)
    wait_sent(ia, 1, some_row)
    swap.wait()

    def local_c():
        rows = c_now[0:local_wins, :]
        for g in range(1, nx):
            rows = jnp.where(xpos == g, c_now[g * local_wins : (g + 1) * local_wins, :], rows)
        return rows

    def step(_, carry):
        a = a_now[...]
        b = b_now[...]
        rows = jnp.concatenate([local_c(), jnp.zeros((LANES - local_wins, LANES), F32)], axis=0)
        cols = jnp.transpose(rows)[:rank]
        weights = [jnp.broadcast_to(cols[:, w : w + 1], (rank, items)) for w in range(local_wins)]
        scaled = jnp.concatenate([a * weight for weight in weights], axis=1)
        s_high, s_low = split(scaled)
        b_high, b_low = split(b)
        sh, sl = s_high.astype(F32), s_low.astype(F32)
        left = jnp.transpose(jnp.concatenate([sh, sh, sl, sl], axis=0)).astype(BF16)
        right = jnp.concatenate([b_high, b_low, b_high, b_low], axis=0)
        model = dot(left, right)
        ratio = cnt[...] / model
        r_high, r_low = split(ratio)

        both = dot(jnp.concatenate([s_high, s_low], axis=0), r_high)
        pb = both[:rank] + both[rank:] + dot(s_high, r_low)
        for q in range(npc):
            g, top = q % groups, (q // groups) * rk_c
            pb_send[q] = pb[top : top + rk_c, g * LANES : (g + 1) * LANES]
        for d in range(1, npc):
            q, device = col_peer(d)
            remote(pb_send.at[q], rc.at[me_c], 3, device).start()
        rc[me_c] = pb_send[me_c]

        bt = jnp.transpose(jnp.concatenate([b_high.astype(F32), b_low.astype(F32)], axis=0))
        bt = bt.astype(BF16)
        back = jnp.transpose(dot(r_high, bt) + dot(r_low, bt))
        back = back[:rank] + back[rank:]
        pa = jnp.zeros((rank, items), F32)
        stats = jnp.zeros((rank, LANES), F32)
        for w in range(local_wins):
            part = back[:, w * items : (w + 1) * items]
            pa = pa + part * weights[w]
            stats = jnp.where(lane_at == w, jnp.sum(part * a, axis=1, keepdims=True), stats)
        stats = jnp.where(lane_at == local_wins, jnp.sum(b, axis=1, keepdims=True), stats)
        stats = jnp.where(lane_at == local_wins + 1, jnp.sum(a, axis=1, keepdims=True), stats)
        stat_rows = jnp.transpose(jnp.concatenate([stats, pad], axis=0))[:8]
        pa_now[...] = pa
        for q in range(npr):
            pa_send[q, 0:8] = stat_rows
            pa_send[q, 8 : 8 + rk_r] = pa_now[q * rk_r : (q + 1) * rk_r, :]
        for d in range(1, npr):
            q, device = row_peer(d)
            remote(pa_send.at[q], rr.at[me_r], 4, device).start()
        rr[me_r] = pa_send[me_r]

        wait_all(rr, 4, some_row)
        total = rr[0, 8 : 8 + rk_r]
        for q in range(1, npr):
            total = total + rr[q, 8 : 8 + rk_r]
        ga[me_r] = total
        for g in range(nx):
            parts = [rr[c * nwin + 2 * g + k, 0:8] for c in range(ncol) for k in range(2)]
            zs[row, g * 8 : (g + 1) * 8] = functools.reduce(jnp.add, parts)
        for d in range(1, npr):
            remote(ga.at[me_r], ga.at[me_r], 5, row_peer(d)[1]).start()

        wait_all(rc, 3, some_col)
        for d in range(1, nrow):
            remote(zs.at[row], zs.at[row], 6, z_peer(d)[1]).start()
        total = rc[0]
        for q in range(1, npc):
            total = total + rc[q]
        gb[me_c] = total
        for d in range(1, npc):
            remote(gb.at[me_c], gb.at[me_c], 7, col_peer(d)[1]).start()

        wait_all(zs, 6, some_z)
        stat = zs[0]
        for q in range(1, nrow):
            stat = stat + zs[q]
        sum_b = stat[local_wins : local_wins + 1] * (1.0 / nrow)
        sum_a = stat[local_wins + 1 : local_wins + 2] * (1.0 / (2 * ncol))
        wins_now = c_now[...]
        sum_c = jnp.sum(wins_now, axis=0, keepdims=True)
        for g in range(nx):
            old = c_now[g * local_wins : (g + 1) * local_wins, :]
            terms = old * stat[g * 8 : g * 8 + local_wins]
            valid = lax.broadcasted_iota(jnp.int32, (local_wins, LANES), 1) < rank
            c_now[g * local_wins : (g + 1) * local_wins, :] = jnp.where(
                valid, old * (0.5 + 0.5 * terms / (sum_a * sum_b)), 0.0
            )
        norm_a = 0.5 / (sum_b * sum_c)
        norm_b = 0.5 / (sum_a * sum_c)
        norms = jnp.where(row_at == 0, norm_a, jnp.where(row_at == 1, norm_b, 0.0))
        norms = jnp.transpose(norms)[:rank]
        scale_a[...] = jnp.broadcast_to(norms[:, 0:1], (rank, items))
        wait_all(ga, 5, some_row)
        for q in range(npr):
            at = slice(q * rk_r, (q + 1) * rk_r)
            a_now[at, :] = a_now[at, :] * (0.5 + scale_a[at, :] * ga[q])
        scale_a[...] = jnp.broadcast_to(norms[:, 1:2], (rank, items))
        wait_all(gb, 7, some_col)
        for q in range(npc):
            g, top = q % groups, (q // groups) * rk_c
            at, over = slice(top, top + rk_c), slice(g * LANES, (g + 1) * LANES)
            b_now[at, over] = b_now[at, over] * (0.5 + scale_a[at, :] * gb[q])

        wait_sent(pb_send, 3, some_col)
        wait_sent(pa_send, 4, some_row)
        wait_sent(ga, 5, some_row)
        wait_sent(zs, 6, some_z)
        wait_sent(gb, 7, some_col)
        return carry

    lax.fori_loop(0, STEPS, step, 0)

    shift = (LANES - me_r * row_width) % LANES
    row_out[...] = pltpu.roll(a_now[...], shift, 1)[:, :row_width]
    block = b_now[:, 0:LANES]
    for g in range(1, groups):
        block = jnp.where(me_c // per == g, b_now[:, g * LANES : (g + 1) * LANES], block)
    shift = (LANES - (me_c % per) * col_width) % LANES
    col_out[...] = pltpu.roll(block, shift, 1)[:, :col_width]
    all_wins = nwin * own_wins
    rows = jnp.concatenate([c_now[...], jnp.zeros((LANES - all_wins, LANES), F32)], axis=0)
    cols = jnp.transpose(rows)[:rank]
    win_out[...] = pltpu.roll(cols, (LANES - win * own_wins) % LANES, 1)[:, :own_wins]


def local(sizes, counts, rows, cols, wins):
    nrow, ncol, nwin = sizes
    rank, row_width = rows.shape
    own_wins, items, columns = counts.shape
    half = columns // 2
    nx = nwin // 2
    npr, npc = ncol * nwin, nrow * nx
    rk_r, rk_c = rank // npr, rank * (half // LANES) // npc
    vmem = lambda *shape: pltpu.VMEM(shape, F32)
    spec = pl.BlockSpec(memory_space=pltpu.VMEM)
    return pl.pallas_call(
        functools.partial(kernel, sizes),
        out_shape=[jax.ShapeDtypeStruct(v.shape, F32) for v in (rows, cols, wins)],
        in_specs=[spec] * 4,
        out_specs=[spec] * 3,
        scratch_shapes=[
            vmem(2 * own_wins * items, half),
            vmem(own_wins * items, half),
            vmem(rank, items),
            vmem(rank, half),
            vmem(nwin * own_wins, LANES),
            vmem(rank, items),
            vmem(rank, items),
            vmem(npr, rank, LANES),
            vmem(npc, rank, LANES),
            vmem(npr, 8 + rk_r, LANES),
            vmem(npr, 8 + rk_r, LANES),
            vmem(npc, rk_c, LANES),
            vmem(npc, rk_c, LANES),
            vmem(npr, rk_r, LANES),
            vmem(npc, rk_c, LANES),
            vmem(nrow, 8 * nx, LANES),
            pltpu.SemaphoreType.DMA((2, 8)),
        ],
        compiler_params=pltpu.CompilerParams(
            collective_id=0, has_side_effects=True, vmem_limit_bytes=40 * 1024 * 1024
        ),
    )(counts, rows, cols, wins)


def solution(mesh):
    in_specs = (
        P("win", "row", "col"),
        P(None, ("row", "col", "win")),
        P(None, ("col", "row", "win")),
        P(None, "win"),
    )
    out_specs = (P(None, ("row", "col", "win")), P(None, ("col", "row", "win")), P(None, "win"))
    sizes = (mesh.shape["row"], mesh.shape["col"], mesh.shape["win"])
    return jax.shard_map(
        functools.partial(local, sizes), mesh=mesh, in_specs=in_specs, out_specs=out_specs, check_vma=False
    )
```

```python
import functools

import jax
import jax.numpy as jnp
from jax import lax
from jax.experimental import pallas as pl
from jax.experimental.pallas import tpu as pltpu
from jax.sharding import PartitionSpec as P

STEPS = 4
LANES = 128
MESH = pl.DeviceIdType.MESH
F32 = jnp.float32
BF16 = jnp.bfloat16


def dot(a, b):
    return lax.dot_general(a, b, (((1,), (0,)), ((), ())), preferred_element_type=F32)


def split(value):
    high = value.astype(BF16)
    low = (value - high.astype(F32)).astype(BF16)
    return high, low


def kernel(
    sizes,
    counts_ref, row_ref, col_ref, win_ref,
    row_out, col_out, win_out,
    counts_here, cnt, cnt_send, a_now, b_now, c_now, cols_now, left_now, high_now, low_now, tile,
    ia, ib, rr, pb_send, rc, gb, zs,
    sems, load_sem,
):
    nrow, ncol, nwin = sizes
    row_width, rank = row_ref.shape
    col_width = col_ref.shape[1]
    own_wins, items, columns = counts_ref.shape
    half = columns // 2
    nx = nwin // 2
    npr, npc = ncol * nwin, nrow * nx
    groups = half // LANES
    first_row, owner_rows = nrow // 4, nrow // 2
    npo = owner_rows * nx
    rk_c = rank * groups // npo
    local_wins = 2 * own_wins

    row, col, win = lax.axis_index("row"), lax.axis_index("col"), lax.axis_index("win")
    xpos, core = win // 2, win % 2
    me_r = col * nwin + win
    me_c = row * nx + xpos
    me_o = me_c - first_row * nx
    is_owner = jnp.logical_and(me_o >= 0, me_o < npo)
    not_owner = jnp.logical_not(is_owner)

    def row_peer(d):
        q = (me_r + d) % npr
        return q, (row, q // nwin, q % nwin)

    def col_peer(d):
        q = (me_c + d) % npc
        return q, (q // nx, col, (q % nx) * 2 + core)

    def z_peer(d):
        q = (row + d) % nrow
        return q, (q, col, win)

    def remote(src, dst, kind, device):
        return pltpu.make_async_remote_copy(
            src_ref=src, dst_ref=dst, send_sem=sems.at[0, kind], recv_sem=sems.at[1, kind],
            device_id=device, device_id_type=MESH,
        )

    def wait_all(slots, kind, device, n=None):
        part = slots.at[pl.ds(0, slots.shape[0] - 1 if n is None else n)]
        remote(part, part, kind, device).wait_recv()

    def wait_sent(slots, kind, device, n=None):
        part = slots.at[pl.ds(0, slots.shape[0] - 1 if n is None else n)]
        remote(part, part, kind, device).wait_send()

    some_row, some_col, some_z = row_peer(1)[1], col_peer(1)[1], z_peer(1)[1]
    partner = (row, col, 2 * xpos + (1 - core))

    barrier = pltpu.get_barrier_semaphore()
    for d in range(1, npr):
        pl.semaphore_signal(barrier, inc=1, device_id=row_peer(d)[1], device_id_type=MESH)
    for d in range(1, npc):
        pl.semaphore_signal(barrier, inc=1, device_id=col_peer(d)[1], device_id_type=MESH)

    load = pltpu.make_async_copy(counts_ref, counts_here, load_sem)
    load.start()
    tile[...] = jnp.zeros((LANES, LANES), F32)
    tile[0:row_width, 0:rank] = row_ref[...]
    tile[row_width : row_width + own_wins, 0:rank] = win_ref[...]
    ia[me_r] = jnp.transpose(tile[...])[:rank]
    ib[me_c] = jnp.zeros((rank, LANES), F32)
    ib[me_c, :, 0:col_width] = col_ref[...]

    pl.semaphore_wait(barrier, npr - 1 + npc - 1)

    for d in range(1, npc):
        remote(ib.at[me_c], ib.at[me_c], 0, col_peer(d)[1]).start()
    for d in range(1, npr):
        remote(ia.at[me_r], ia.at[me_r], 1, row_peer(d)[1]).start()

    span = 2 * LANES
    src_at = lax.broadcasted_iota(jnp.int32, (span, span), 0)
    dst_at = lax.broadcasted_iota(jnp.int32, (span, span), 1)
    side = dst_at // LANES
    lane = dst_at % LANES
    take = jnp.where(side == 0, core, 1 - core)
    origin = (lane // col_width) * (2 * col_width) + take * col_width + lane % col_width
    order = jnp.where(src_at == origin, 1.0, 0.0).astype(BF16)
    base = core * (own_wins * items)
    load.wait()
    for w in range(own_wins):
        for g in range(groups):
            block = counts_here[w, :, g * span : (g + 1) * span].astype(F32).astype(BF16)
            moved = dot(block, order)
            at = pl.ds(pl.multiple_of(base + w * items, items), items)
            cnt[at, g * LANES : (g + 1) * LANES] = moved[:, :LANES]
            cnt_send[w * items : (w + 1) * items, g * LANES : (g + 1) * LANES] = moved[:, LANES:]
    mine = cnt.at[pl.ds(pl.multiple_of(base, items), own_wins * items)]
    swap = remote(cnt_send, mine, 8, partner)
    swap.start()

    lane_at = lax.broadcasted_iota(jnp.int32, (rank, LANES), 1)
    row_at = lax.broadcasted_iota(jnp.int32, (LANES, LANES), 0)

    wait_all(ib, 0, some_col)
    per = LANES // col_width
    for g in range(groups):
        block = ib[g * per]
        for m in range(1, per):
            moved = pltpu.roll(ib[g * per + m], m * col_width, 1)
            block = jnp.where(lane_at // col_width == m, moved, block)
        b_now[:, g * LANES : (g + 1) * LANES] = block
    wait_all(ia, 1, some_row)
    block = ia[0]
    for m in range(1, npr):
        moved = pltpu.roll(ia[m], m * row_width, 1)
        block = jnp.where(lane_at // row_width == m, moved, block)
    a_now[...] = block
    wins = jnp.zeros((rank, LANES), F32)
    for w in range(nwin):
        moved = pltpu.roll(ia[w], (LANES - row_width + w * own_wins) % LANES, 1)
        wins = jnp.where(lane_at // own_wins == w, moved, wins)
    pad = jnp.zeros((LANES - rank, LANES), F32)
    c_now[...] = jnp.transpose(jnp.concatenate([wins, pad], axis=0))[: nwin * own_wins]
    wait_sent(ib, 0, some_col)
    wait_sent(ia, 1, some_row)
    swap.wait()

    def local_c():
        rows = c_now[0:local_wins, :]
        for g in range(1, nx):
            rows = jnp.where(xpos == g, c_now[g * local_wins : (g + 1) * local_wins, :], rows)
        return rows

    def put_cols(extra):
        rows = jnp.concatenate([local_c(), jnp.zeros((LANES - local_wins, LANES), F32)], axis=0)
        rows = jnp.where(row_at == local_wins, extra, rows)
        cols_now[...] = jnp.transpose(rows)[:rank]

    def weight(w):
        return jnp.broadcast_to(cols_now[:, w : w + 1], (rank, items))

    def prepare():
        a = a_now[...]
        scaled = jnp.concatenate([a * weight(w) for w in range(local_wins)], axis=1)
        s_high, s_low = split(scaled)
        sh, sl = s_high.astype(F32), s_low.astype(F32)
        left_now[...] = jnp.transpose(jnp.concatenate([sh, sh, sl, sl], axis=0)).astype(BF16)
        high_now[...] = s_high
        low_now[...] = s_low

    def step(index, carry):
        odd = index % 2
        k_rr, k_zs = 4 + odd, 6 + odd
        b = b_now[...]
        b_high, b_low = split(b)
        right = jnp.concatenate([b_high, b_low, b_high, b_low], axis=0)
        ratio = cnt[...] / dot(left_now[...], right)
        r_high, r_low = split(ratio)

        s_high = high_now[...]
        both = dot(jnp.concatenate([s_high, low_now[...]], axis=0), r_high)
        pb = both[:rank] + both[rank:] + dot(s_high, r_low)
        for o in range(npo):
            g, top = o % groups, (o // groups) * rk_c
            pb_send[o] = pb[top : top + rk_c, g * LANES : (g + 1) * LANES]
        for o in range(npo):

            @pl.when(me_o != o)
            def _(o=o):
                device = (first_row + o // nx, col, (o % nx) * 2 + core)
                remote(pb_send.at[o], rc.at[me_c], 3, device).start()

        a = a_now[...]
        bt = jnp.transpose(jnp.concatenate([b_high.astype(F32), b_low.astype(F32)], axis=0))
        bt = bt.astype(BF16)
        back = jnp.transpose(dot(r_high, bt) + dot(r_low, bt))
        back = back[:rank] + back[rank:]
        pa = jnp.zeros((rank, items), F32)
        stats = jnp.zeros((rank, LANES), F32)
        for w in range(local_wins):
            part = back[:, w * items : (w + 1) * items]
            pa = pa + part * weight(w)
            stats = jnp.where(lane_at == w, jnp.sum(part * a, axis=1, keepdims=True), stats)
        stats = jnp.where(lane_at == local_wins, jnp.sum(b, axis=1, keepdims=True), stats)
        stats = jnp.where(lane_at == local_wins + 1, jnp.sum(a, axis=1, keepdims=True), stats)
        rr[odd, me_r, 0:rank] = pa
        rr[odd, me_r, rank : rank + 8] = jnp.transpose(jnp.concatenate([stats, pad], axis=0))[:8]
        for d in range(1, npr):
            remote(rr.at[odd, me_r], rr.at[odd, me_r], k_rr, row_peer(d)[1]).start()

        @pl.when(is_owner)
        def _():
            rc[me_c] = pb_send[me_o]
            wait_all(rc, 3, some_col)
            total = rc[0]
            for q in range(1, npc):
                total = total + rc[q]
            gb[me_o] = total
            for d in range(1, npc):
                remote(gb.at[me_o], gb.at[me_o], 2, col_peer(d)[1]).start()

        wait_all(rr.at[odd], k_rr, some_row)
        for g in range(nx):
            parts = [rr[odd, c * nwin + 2 * g + k, rank : rank + 8] for c in range(ncol) for k in range(2)]
            zs[odd, row, g * 8 : (g + 1) * 8] = functools.reduce(jnp.add, parts)
        for d in range(1, nrow):
            remote(zs.at[odd, row], zs.at[odd, row], k_zs, z_peer(d)[1]).start()

        sum_c = jnp.sum(c_now[...], axis=0, keepdims=True)
        sum_b = zs[odd, row, local_wins : local_wins + 1]
        rows = jnp.where(row_at == 0, 0.5 / (sum_b * sum_c), 0.0)
        norm_a = jnp.broadcast_to(jnp.transpose(rows)[:rank, 0:1], (rank, items))
        total = rr[odd, 0, 0:rank]
        for q in range(1, npr):
            total = total + rr[odd, q, 0:rank]
        a_now[...] = a * (0.5 + norm_a * total)

        wait_all(zs.at[odd], k_zs, some_z)
        stat = zs[odd, 0]
        for q in range(1, nrow):
            stat = stat + zs[odd, q]
        sum_b = stat[local_wins : local_wins + 1] * (1.0 / nrow)
        sum_a = stat[local_wins + 1 : local_wins + 2] * (1.0 / (2 * ncol))
        norm_c = 0.5 / (sum_a * sum_b)
        valid = lax.broadcasted_iota(jnp.int32, (local_wins, LANES), 1) < rank
        for g in range(nx):
            at = slice(g * local_wins, (g + 1) * local_wins)
            old = c_now[at, :]
            terms = old * stat[g * 8 : g * 8 + local_wins]
            c_now[at, :] = jnp.where(valid, old * (0.5 + norm_c * terms), 0.0)
        put_cols(0.5 / (sum_a * sum_c))
        norm_b = jnp.broadcast_to(cols_now[:, local_wins : local_wins + 1], (rank, items))
        tile[0:rank, :] = norm_b
        prepare()

        @pl.when(is_owner)
        def _():
            wait_all(gb, 2, some_col, npo - 1)

        @pl.when(not_owner)
        def _():
            wait_all(gb, 2, some_col, npo)

        for o in range(npo):
            g, top = o % groups, (o // groups) * rk_c
            at, over = slice(top, top + rk_c), slice(g * LANES, (g + 1) * LANES)
            b_now[at, over] = b_now[at, over] * (0.5 + tile[at, :] * gb[o])

        @pl.when(is_owner)
        def _():
            wait_sent(pb_send, 3, some_col, npo - 1)
            wait_sent(rc, 2, some_col)

        @pl.when(not_owner)
        def _():
            wait_sent(pb_send, 3, some_col, npo)

        wait_sent(rr.at[odd], k_rr, some_row)
        wait_sent(zs.at[odd], k_zs, some_z)
        return carry

    put_cols(jnp.zeros((1, LANES), F32))
    prepare()
    lax.fori_loop(0, STEPS, step, 0)

    shift = (LANES - me_r * row_width) % LANES
    rows = jnp.concatenate([pltpu.roll(a_now[...], shift, 1), pad], axis=0)
    row_out[...] = jnp.transpose(rows)[:row_width, :rank]
    block = b_now[:, 0:LANES]
    for g in range(1, groups):
        block = jnp.where(me_c // per == g, b_now[:, g * LANES : (g + 1) * LANES], block)
    shift = (LANES - (me_c % per) * col_width) % LANES
    col_out[...] = pltpu.roll(block, shift, 1)[:, :col_width]
    win_out[...] = c_now[pl.ds(win * own_wins, own_wins), :][:, :rank]


def local(sizes, counts, rows, cols, wins):
    nrow, ncol, nwin = sizes
    rank, row_width = rows.shape
    own_wins, items, columns = counts.shape
    half = columns // 2
    nx = nwin // 2
    npr, npc = ncol * nwin, nrow * nx
    npo = (nrow // 2) * nx
    rk_c = rank * (half // LANES) // npo
    vmem = lambda *shape, dtype=F32: pltpu.VMEM(shape, dtype)
    spec = pl.BlockSpec(memory_space=pltpu.VMEM)
    args = (counts, rows.T, cols, wins.T)
    out = pl.pallas_call(
        functools.partial(kernel, sizes),
        out_shape=[jax.ShapeDtypeStruct(v.shape, F32) for v in args[1:]],
        in_specs=[pl.BlockSpec(memory_space=pl.ANY)] + [spec] * 3,
        out_specs=[spec] * 3,
        scratch_shapes=[
            vmem(*counts.shape, dtype=jnp.int32),
            vmem(2 * own_wins * items, half),
            vmem(own_wins * items, half),
            vmem(rank, items),
            vmem(rank, half),
            vmem(nwin * own_wins, LANES),
            vmem(rank, LANES),
            vmem(2 * own_wins * items, 4 * rank, dtype=BF16),
            vmem(rank, 2 * own_wins * items, dtype=BF16),
            vmem(rank, 2 * own_wins * items, dtype=BF16),
            vmem(LANES, LANES),
            vmem(npr, rank, LANES),
            vmem(npc, rank, LANES),
            vmem(2, npr, rank + 8, LANES),
            vmem(npo, rk_c, LANES),
            vmem(npc, rk_c, LANES),
            vmem(npo, rk_c, LANES),
            vmem(2, nrow, 8 * nx, LANES),
            pltpu.SemaphoreType.DMA((2, 9)),
            pltpu.SemaphoreType.DMA,
        ],
        compiler_params=pltpu.CompilerParams(
            collective_id=0, has_side_effects=True, vmem_limit_bytes=60 * 1024 * 1024
        ),
    )(*args)
    return out[0].T, out[1], out[2].T


def solution(mesh):
    in_specs = (
        P("win", "row", "col"),
        P(None, ("row", "col", "win")),
        P(None, ("col", "row", "win")),
        P(None, "win"),
    )
    out_specs = (P(None, ("row", "col", "win")), P(None, ("col", "row", "win")), P(None, "win"))
    sizes = (mesh.shape["row"], mesh.shape["col"], mesh.shape["win"])
    return jax.shard_map(
        functools.partial(local, sizes), mesh=mesh, in_specs=in_specs, out_specs=out_specs, check_vma=False
    )
```

```python
import functools

import jax
import jax.numpy as jnp
from jax import lax
from jax.experimental import pallas as pl
from jax.experimental.pallas import tpu as pltpu
from jax.sharding import PartitionSpec as P

STEPS = 4
LANES = 128
MESH = pl.DeviceIdType.MESH
F32 = jnp.float32
BF16 = jnp.bfloat16


def dot(a, b):
    return lax.dot_general(a, b, (((1,), (0,)), ((), ())), preferred_element_type=F32)


def split(value):
    high = value.astype(BF16)
    low = (value - high.astype(F32)).astype(BF16)
    return high, low


def kernel(
    sizes,
    counts_ref, row_ref, col_ref, win_ref,
    row_out, col_out, win_out,
    counts_here, cnt, cnt_send, a_now, b_now, c_now, cols_now, left_now, high_now, low_now, tile,
    ia, ib, rr, sr, pb_send, rc, gb, zs,
    sems, load_sem,
):
    nrow, ncol, nwin = sizes
    row_width, rank = row_ref.shape
    col_width = col_ref.shape[1]
    own_wins, items, columns = counts_ref.shape
    half = columns // 2
    nx = nwin // 2
    npr, npc = ncol * nwin, nrow * nx
    groups = half // LANES
    first_row, owner_rows = nrow // 4, nrow // 2
    npo = owner_rows * nx
    rk_c = rank * groups // npo
    local_wins = 2 * own_wins

    row, col, win = lax.axis_index("row"), lax.axis_index("col"), lax.axis_index("win")
    xpos, core = win // 2, win % 2
    me_r = col * nwin + win
    me_c = row * nx + xpos
    me_o = me_c - first_row * nx
    is_owner = jnp.logical_and(me_o >= 0, me_o < npo)
    not_owner = jnp.logical_not(is_owner)

    def row_peer(d):
        q = (me_r + d) % npr
        return q, (row, q // nwin, q % nwin)

    def col_peer(d):
        q = (me_c + d) % npc
        return q, (q // nx, col, (q % nx) * 2 + core)

    def z_peer(d):
        q = (row + d) % nrow
        return q, (q, col, win)

    def remote(src, dst, kind, device):
        return pltpu.make_async_remote_copy(
            src_ref=src, dst_ref=dst, send_sem=sems.at[0, kind], recv_sem=sems.at[1, kind],
            device_id=device, device_id_type=MESH,
        )

    def wait_all(slots, kind, device, n=None):
        part = slots.at[pl.ds(0, slots.shape[0] - 1 if n is None else n)]
        remote(part, part, kind, device).wait_recv()

    def wait_sent(slots, kind, device, n=None):
        part = slots.at[pl.ds(0, slots.shape[0] - 1 if n is None else n)]
        remote(part, part, kind, device).wait_send()

    some_row, some_col, some_z = row_peer(1)[1], col_peer(1)[1], z_peer(1)[1]
    partner = (row, col, 2 * xpos + (1 - core))

    barrier = pltpu.get_barrier_semaphore()
    for d in range(1, npr):
        pl.semaphore_signal(barrier, inc=1, device_id=row_peer(d)[1], device_id_type=MESH)
    for d in range(1, npc):
        pl.semaphore_signal(barrier, inc=1, device_id=col_peer(d)[1], device_id_type=MESH)

    load = pltpu.make_async_copy(counts_ref, counts_here, load_sem)
    load.start()
    tile[...] = jnp.zeros((LANES, LANES), F32)
    tile[0:row_width, 0:rank] = row_ref[...]
    tile[row_width : row_width + own_wins, 0:rank] = win_ref[...]
    ia[me_r] = jnp.transpose(tile[...])[:rank]
    ib[me_c] = jnp.zeros((rank, LANES), F32)
    ib[me_c, :, 0:col_width] = col_ref[...]

    span = 2 * LANES
    src_at = lax.broadcasted_iota(jnp.int32, (span, span), 0)
    dst_at = lax.broadcasted_iota(jnp.int32, (span, span), 1)
    side = dst_at // LANES
    lane = dst_at % LANES
    take = jnp.where(side == 0, core, 1 - core)
    origin = (lane // col_width) * (2 * col_width) + take * col_width + lane % col_width
    order = jnp.where(src_at == origin, 1.0, 0.0).astype(BF16)
    base = core * (own_wins * items)
    load.wait()
    for w in range(own_wins):
        for g in range(groups):
            block = counts_here[w, :, g * span : (g + 1) * span].astype(F32).astype(BF16)
            moved = dot(block, order)
            at = pl.ds(pl.multiple_of(base + w * items, items), items)
            cnt[at, g * LANES : (g + 1) * LANES] = moved[:, :LANES]
            cnt_send[w * items : (w + 1) * items, g * LANES : (g + 1) * LANES] = moved[:, LANES:]
    pl.semaphore_wait(barrier, npr - 1 + npc - 1)

    for d in range(1, npc):
        remote(ib.at[me_c], ib.at[me_c], 0, col_peer(d)[1]).start()
    for d in range(1, npr):
        remote(ia.at[me_r], ia.at[me_r], 1, row_peer(d)[1]).start()

    mine = cnt.at[pl.ds(pl.multiple_of(base, items), own_wins * items)]
    swap = remote(cnt_send, mine, 8, partner)
    swap.start()

    lane_at = lax.broadcasted_iota(jnp.int32, (rank, LANES), 1)
    row_at = lax.broadcasted_iota(jnp.int32, (LANES, LANES), 0)

    wait_all(ib, 0, some_col)
    per = LANES // col_width
    for g in range(groups):
        block = ib[g * per]
        for m in range(1, per):
            moved = pltpu.roll(ib[g * per + m], m * col_width, 1)
            block = jnp.where(lane_at // col_width == m, moved, block)
        b_now[:, g * LANES : (g + 1) * LANES] = block
    wait_all(ia, 1, some_row)
    block = ia[0]
    for m in range(1, npr):
        moved = pltpu.roll(ia[m], m * row_width, 1)
        block = jnp.where(lane_at // row_width == m, moved, block)
    a_now[...] = block
    wins = jnp.zeros((rank, LANES), F32)
    for w in range(nwin):
        moved = pltpu.roll(ia[w], (LANES - row_width + w * own_wins) % LANES, 1)
        wins = jnp.where(lane_at // own_wins == w, moved, wins)
    pad = jnp.zeros((LANES - rank, LANES), F32)
    c_now[...] = jnp.transpose(jnp.concatenate([wins, pad], axis=0))[: nwin * own_wins]
    wait_sent(ib, 0, some_col)
    wait_sent(ia, 1, some_row)
    swap.wait()

    def local_c():
        rows = c_now[0:local_wins, :]
        for g in range(1, nx):
            rows = jnp.where(xpos == g, c_now[g * local_wins : (g + 1) * local_wins, :], rows)
        return rows

    def put_cols(extra):
        rows = jnp.concatenate([local_c(), jnp.zeros((LANES - local_wins, LANES), F32)], axis=0)
        rows = jnp.where(row_at == local_wins, extra, rows)
        cols_now[...] = jnp.transpose(rows)[:rank]

    def weight(w):
        return jnp.broadcast_to(cols_now[:, w : w + 1], (rank, items))

    def prepare():
        a = a_now[...]
        scaled = jnp.concatenate([a * weight(w) for w in range(local_wins)], axis=1)
        s_high, s_low = split(scaled)
        sh, sl = s_high.astype(F32), s_low.astype(F32)
        left_now[...] = jnp.transpose(jnp.concatenate([sh, sh, sl, sl], axis=0)).astype(BF16)
        high_now[...] = s_high
        low_now[...] = s_low

    def step(index, carry):
        odd = index % 2
        k_rr, k_zs, k_sr = 4 + odd, 6 + odd, 9 + odd
        b = b_now[...]
        b_high, b_low = split(b)
        right = jnp.concatenate([b_high, b_low, b_high, b_low], axis=0)
        ratio = cnt[...] / dot(left_now[...], right)
        r_high, r_low = split(ratio)

        s_high = high_now[...]
        both = dot(jnp.concatenate([s_high, low_now[...]], axis=0), r_high)
        pb = both[:rank] + both[rank:] + dot(s_high, r_low)
        for o in range(npo):
            g, top = o % groups, (o // groups) * rk_c
            pb_send[o] = pb[top : top + rk_c, g * LANES : (g + 1) * LANES]
        for o in range(npo):

            @pl.when(me_o != o)
            def _(o=o):
                device = (first_row + o // nx, col, (o % nx) * 2 + core)
                remote(pb_send.at[o], rc.at[me_c], 3, device).start()

        a = a_now[...]
        bt = jnp.transpose(jnp.concatenate([b_high.astype(F32), b_low.astype(F32)], axis=0))
        bt = bt.astype(BF16)
        back = jnp.transpose(dot(r_high, bt) + dot(r_low, bt))
        back = back[:rank] + back[rank:]
        pa = jnp.zeros((rank, items), F32)
        stats = jnp.zeros((rank, LANES), F32)
        for w in range(local_wins):
            part = back[:, w * items : (w + 1) * items]
            pa = pa + part * weight(w)
            stats = jnp.where(lane_at == w, jnp.sum(part * a, axis=1, keepdims=True), stats)
        stats = jnp.where(lane_at == local_wins, jnp.sum(b, axis=1, keepdims=True), stats)
        stats = jnp.where(lane_at == local_wins + 1, jnp.sum(a, axis=1, keepdims=True), stats)
        sr[odd, me_r] = jnp.transpose(jnp.concatenate([stats, pad], axis=0))[:8]
        for d in range(1, npr):
            remote(sr.at[odd, me_r], sr.at[odd, me_r], k_sr, row_peer(d)[1]).start()
        rr[odd, me_r] = pa
        for d in range(1, npr):
            remote(rr.at[odd, me_r], rr.at[odd, me_r], k_rr, row_peer(d)[1]).start()

        @pl.when(is_owner)
        def _():
            rc[me_c] = pb_send[me_o]
            wait_all(rc, 3, some_col)
            total = rc[0]
            for q in range(1, npc):
                total = total + rc[q]
            gb[me_o] = total
            for d in range(1, npc):
                remote(gb.at[me_o], gb.at[me_o], 2, col_peer(d)[1]).start()

        wait_all(sr.at[odd], k_sr, some_row)
        for g in range(nx):
            parts = [sr[odd, c * nwin + 2 * g + k] for c in range(ncol) for k in range(2)]
            zs[odd, row, g * 8 : (g + 1) * 8] = functools.reduce(jnp.add, parts)
        for d in range(1, nrow):
            remote(zs.at[odd, row], zs.at[odd, row], k_zs, z_peer(d)[1]).start()

        sum_c = jnp.sum(c_now[...], axis=0, keepdims=True)
        sum_b = zs[odd, row, local_wins : local_wins + 1]
        rows = jnp.where(row_at == 0, 0.5 / (sum_b * sum_c), 0.0)
        norm_a = jnp.broadcast_to(jnp.transpose(rows)[:rank, 0:1], (rank, items))
        wait_all(rr.at[odd], k_rr, some_row)
        total = rr[odd, 0]
        for q in range(1, npr):
            total = total + rr[odd, q]
        a_now[...] = a * (0.5 + norm_a * total)

        wait_all(zs.at[odd], k_zs, some_z)
        stat = zs[odd, 0]
        for q in range(1, nrow):
            stat = stat + zs[odd, q]
        sum_b = stat[local_wins : local_wins + 1] * (1.0 / nrow)
        sum_a = stat[local_wins + 1 : local_wins + 2] * (1.0 / (2 * ncol))
        norm_c = 0.5 / (sum_a * sum_b)
        valid = lax.broadcasted_iota(jnp.int32, (local_wins, LANES), 1) < rank
        for g in range(nx):
            at = slice(g * local_wins, (g + 1) * local_wins)
            old = c_now[at, :]
            terms = old * stat[g * 8 : g * 8 + local_wins]
            c_now[at, :] = jnp.where(valid, old * (0.5 + norm_c * terms), 0.0)
        put_cols(0.5 / (sum_a * sum_c))
        norm_b = jnp.broadcast_to(cols_now[:, local_wins : local_wins + 1], (rank, items))
        tile[0:rank, :] = norm_b
        prepare()

        @pl.when(is_owner)
        def _():
            wait_all(gb, 2, some_col, npo - 1)

        @pl.when(not_owner)
        def _():
            wait_all(gb, 2, some_col, npo)

        for o in range(npo):
            g, top = o % groups, (o // groups) * rk_c
            at, over = slice(top, top + rk_c), slice(g * LANES, (g + 1) * LANES)
            b_now[at, over] = b_now[at, over] * (0.5 + tile[at, :] * gb[o])

        @pl.when(is_owner)
        def _():
            wait_sent(pb_send, 3, some_col, npo - 1)
            wait_sent(rc, 2, some_col)

        @pl.when(not_owner)
        def _():
            wait_sent(pb_send, 3, some_col, npo)

        wait_sent(rr.at[odd], k_rr, some_row)
        wait_sent(sr.at[odd], k_sr, some_row)
        wait_sent(zs.at[odd], k_zs, some_z)
        return carry

    put_cols(jnp.zeros((1, LANES), F32))
    prepare()
    lax.fori_loop(0, STEPS, step, 0)

    shift = (LANES - me_r * row_width) % LANES
    rows = jnp.concatenate([pltpu.roll(a_now[...], shift, 1), pad], axis=0)
    row_out[...] = jnp.transpose(rows)[:row_width, :rank]
    block = b_now[:, 0:LANES]
    for g in range(1, groups):
        block = jnp.where(me_c // per == g, b_now[:, g * LANES : (g + 1) * LANES], block)
    shift = (LANES - (me_c % per) * col_width) % LANES
    col_out[...] = pltpu.roll(block, shift, 1)[:, :col_width]
    win_out[...] = c_now[pl.ds(win * own_wins, own_wins), :][:, :rank]


def hand_on(*refs):
    for source, target in zip(refs[:3], refs[3:]):
        target[...] = source[...]


def local(sizes, counts, rows, cols, wins):
    nrow, ncol, nwin = sizes
    rank, row_width = rows.shape
    own_wins, items, columns = counts.shape
    half = columns // 2
    nx = nwin // 2
    npr, npc = ncol * nwin, nrow * nx
    npo = (nrow // 2) * nx
    rk_c = rank * (half // LANES) // npo
    vmem = lambda *shape, dtype=F32: pltpu.VMEM(shape, dtype)
    spec = pl.BlockSpec(memory_space=pltpu.VMEM)
    args = (counts, rows.T, cols, wins.T)
    out = pl.pallas_call(
        functools.partial(kernel, sizes),
        out_shape=[jax.ShapeDtypeStruct(v.shape, F32) for v in args[1:]],
        in_specs=[pl.BlockSpec(memory_space=pl.ANY)] + [spec] * 3,
        out_specs=[spec] * 3,
        scratch_shapes=[
            vmem(*counts.shape, dtype=jnp.int32),
            vmem(2 * own_wins * items, half),
            vmem(own_wins * items, half),
            vmem(rank, items),
            vmem(rank, half),
            vmem(nwin * own_wins, LANES),
            vmem(rank, LANES),
            vmem(2 * own_wins * items, 4 * rank, dtype=BF16),
            vmem(rank, 2 * own_wins * items, dtype=BF16),
            vmem(rank, 2 * own_wins * items, dtype=BF16),
            vmem(LANES, LANES),
            vmem(npr, rank, LANES),
            vmem(npc, rank, LANES),
            vmem(2, npr, rank, LANES),
            vmem(2, npr, 8, LANES),
            vmem(npo, rk_c, LANES),
            vmem(npc, rk_c, LANES),
            vmem(npo, rk_c, LANES),
            vmem(2, nrow, 8 * nx, LANES),
            pltpu.SemaphoreType.DMA((2, 11)),
            pltpu.SemaphoreType.DMA,
        ],
        compiler_params=pltpu.CompilerParams(
            collective_id=0, has_side_effects=True, vmem_limit_bytes=60 * 1024 * 1024
        ),
    )(*args)
    out = pl.pallas_call(
        hand_on,
        out_shape=[jax.ShapeDtypeStruct(v.shape, F32) for v in args[1:]],
        in_specs=[spec] * 3,
        out_specs=[spec] * 3,
    )(*out)
    return out[0].T, out[1], out[2].T


def solution(mesh):
    in_specs = (
        P("win", "row", "col"),
        P(None, ("row", "col", "win")),
        P(None, ("col", "row", "win")),
        P(None, "win"),
    )
    out_specs = (P(None, ("row", "col", "win")), P(None, ("col", "row", "win")), P(None, "win"))
    sizes = (mesh.shape["row"], mesh.shape["col"], mesh.shape["win"])
    return jax.shard_map(
        functools.partial(local, sizes), mesh=mesh, in_specs=in_specs, out_specs=out_specs, check_vma=False
    )
```
